32 devices in a mesh: ctx: 8 (over y, x, core), fsdp: 4 (over z).
Axes of the slice: x: 2, y: 2, z: 4, core: 2. Of those that a mesh axis runs over, the one named last changes fastest.
Arguments:
- tokens: bfloat16 [4, 2048, 1152], P('fsdp', 'ctx'), may hold values from -6 to 6
- dealing: int32 [4, 8], P('fsdp'), may hold values from 0 to 7, each once within a row
- lengths: int32 [4, 2], P('fsdp'), may hold values from 768 to 1280, as said below
- cotangent: bfloat16 [4, 2048, 1152], P('fsdp', 'ctx'), may hold values from -6 to 6
- query_proj: bfloat16 [1152, 1024], P('fsdp'), may hold values from -0.1875 to 0.1875
- key_proj: bfloat16 [1152, 256], P('fsdp'), may hold values from -0.1875 to 0.1875
- value_proj: bfloat16 [1152, 256], P('fsdp'), may hold values from -0.1875 to 0.1875
- out_proj: bfloat16 [1024, 1152], P('fsdp'), may hold values from -0.1875 to 0.1875
- gate_proj: bfloat16 [1152, 6912], P('fsdp'), may hold values from -0.1875 to 0.1875
- up_proj: bfloat16 [1152, 6912], P('fsdp'), may hold values from -0.1875 to 0.1875
- down_proj: bfloat16 [6912, 1152], P('fsdp'), may hold values from -0.078125 to 0.078125
- gain_input: bfloat16 [1152], P('fsdp'), may hold values from 0.5 to 1.5
- gain_query: bfloat16 [256], P('fsdp'), may hold values from 1 to 2
- gain_key: bfloat16 [256], P('fsdp'), may hold values from 1 to 2
- gain_attn: bfloat16 [1152], P('fsdp'), may hold values from 0.5 to 1.5
- gain_pre: bfloat16 [1152], P('fsdp'), may hold values from 0.5 to 1.5
- gain_post: bfloat16 [1152], P('fsdp'), may hold values from 0.5 to 1.5
Outputs:
- outputs: bfloat16 [4, 2048, 1152], P('fsdp', 'ctx')
- d_tokens: float32 [4, 2048, 1152], P('fsdp', 'ctx')
- grad_query_proj: float32 [1152, 1024], P('fsdp')
- grad_key_proj: float32 [1152, 256], P('fsdp')
- grad_value_proj: float32 [1152, 256], P('fsdp')
- grad_out_proj: float32 [1024, 1152], P('fsdp')
- grad_gate_proj: float32 [1152, 6912], P('fsdp')
- grad_up_proj: float32 [1152, 6912], P('fsdp')
- grad_down_proj: float32 [6912, 1152], P('fsdp')
- grad_gain_input: float32 [1152], P('fsdp')
- grad_gain_query: float32 [256], P('fsdp')
- grad_gain_key: float32 [256], P('fsdp')
- grad_gain_attn: float32 [1152], P('fsdp')
- grad_gain_pre: float32 [1152], P('fsdp')
- grad_gain_post: float32 [1152], P('fsdp')
The draws below stay inside these ranges and needn't reach their ends.
Inputs may be any that keep to these rules, and one draw needn't show every extreme that they name: Each row is a permutation; context index c holds the group's blocks dealing[c] and 15 - dealing[c] of 128 tokens, in that order. The two lengths of a group's sequences in order, summing to 2048; one of them is 1280, the other 768, in either order.
All inputs are finite; a program needn't handle non-finite values.
Results may differ from the reference program's by a relative error of at most 0.025.
Values may be sent and summed in bfloat16 or wider, within the bound.
A program may use at most 320 MiB of HBM per device.

```python
import math
import jax
import jax.numpy as jnp
from jax import lax

D = 1152
HD = 256
FF = 6912
TOK_DEV = 256
GROUPS = 4
GROUP_TOK = 2048
LONGEST = 1280
HQ = 1024
N_CTX = 8


def draw_lengths(key, part):
    key = jax.random.fold_in(key, 11)
    flipped = jax.random.randint(key, (GROUPS,), 0, 2).astype(jnp.int32)
    longer = jnp.full((GROUPS,), LONGEST, jnp.int32)
    shorter = jnp.full((GROUPS,), GROUP_TOK - LONGEST, jnp.int32)
    first_len = jnp.where(flipped == 1, longer, shorter)
    second_len = jnp.where(flipped == 1, shorter, longer)
    return jnp.stack([first_len, second_len], axis=1).astype(jnp.int32)


def level_of(key, shape, cuts, smallest, top_value):
    level, own = 1.0, jax.random.fold_in(key, 6)
    for dim, parts in cuts:
        draws = jnp.exp(jax.random.uniform(jax.random.fold_in(own, dim), (parts,), jnp.float32, smallest / len(cuts), top_value / len(cuts)))
        level = level * jnp.repeat(draws, shape[dim] // parts).reshape([-1 if axis == dim else 1 for axis in range(len(shape))])
    return level


def centred(stream_key, shape, width, bound, shards=(), kind=jnp.bfloat16):
    drawn = jax.random.normal(stream_key, shape, jnp.float32) * width
    if len(shards) > 0:
        drawn = level_of(stream_key, shape, shards, -0.22, 0.18) * drawn
    return jnp.clip(drawn, min=-bound, max=bound).astype(kind)


def setup_inputs(seed: int = 0) -> dict:
    seeds = jax.random.split(jax.random.key(seed), 18)
    return {
        "tokens": centred(seeds[0], (GROUPS, GROUP_TOK, D), 1.0, 6.0, ((0, 4), (1, 8))),
        "dealing": jax.vmap(lambda own: jax.random.permutation(own, N_CTX))(jax.random.split(seeds[1], GROUPS)).reshape((GROUPS, N_CTX)).astype(jnp.int32),
        "lengths": draw_lengths(jax.random.fold_in(seeds[17], 71), 0),
        "cotangent": centred(seeds[3], (GROUPS, GROUP_TOK, D), 1.0, 6.0, ((0, 4), (1, 8))),
        "query_proj": centred(seeds[4], (D, HQ), D ** -0.5, 0.1875, ((0, 4),)),
        "key_proj": centred(seeds[5], (D, HD), D ** -0.5, 0.1875, ((0, 4),)),
        "value_proj": centred(seeds[6], (D, HD), D ** -0.5, 0.1875, ((0, 4),)),
        "out_proj": centred(seeds[7], (HQ, D), HQ ** -0.5, 0.1875, ((0, 4),)),
        "gate_proj": centred(seeds[8], (D, FF), D ** -0.5, 0.1875, ((0, 4),)),
        "up_proj": centred(seeds[9], (D, FF), D ** -0.5, 0.1875, ((0, 4),)),
        "down_proj": centred(seeds[10], (FF, D), FF ** -0.5, 0.078125, ((0, 4),)),
        "gain_input": jnp.clip(0.5 + 1.0 * jax.random.uniform(seeds[11], (D,), jnp.float32) ** level_of(seeds[11], (D,), ((0, 4),), -0.2, 0.2), 0.5, 1.5).astype(jnp.bfloat16),
        "gain_query": jnp.clip(1.0 + 1.0 * jax.random.uniform(seeds[12], (HD,), jnp.float32) ** level_of(seeds[12], (HD,), ((0, 4),), -0.2, 0.2), 1.0, 2.0).astype(jnp.bfloat16),
        "gain_key": jnp.clip(1.0 + 1.0 * jax.random.uniform(seeds[13], (HD,), jnp.float32) ** level_of(seeds[13], (HD,), ((0, 4),), -0.2, 0.2), 1.0, 2.0).astype(jnp.bfloat16),
        "gain_attn": jnp.clip(0.5 + 1.0 * jax.random.uniform(seeds[14], (D,), jnp.float32) ** level_of(seeds[14], (D,), ((0, 4),), -0.2, 0.2), 0.5, 1.5).astype(jnp.bfloat16),
        "gain_pre": jnp.clip(0.5 + 1.0 * jax.random.uniform(seeds[15], (D,), jnp.float32) ** level_of(seeds[15], (D,), ((0, 4),), -0.2, 0.2), 0.5, 1.5).astype(jnp.bfloat16),
        "gain_post": jnp.clip(0.5 + 1.0 * jax.random.uniform(seeds[16], (D,), jnp.float32) ** level_of(seeds[16], (D,), ((0, 4),), -0.2, 0.2), 0.5, 1.5).astype(jnp.bfloat16),
    }


EPS = 1e-06
THETA = 1000000.0

@jax.custom_vjp
def low(v):
    return lax.optimization_barrier(v.astype(jnp.bfloat16)).astype(jnp.float32)

@jax.custom_vjp
def low_back(v):
    return v

def low_keep(v):
    return (low(v), None)

def low_pass(kept, grad):
    return (grad,)

def back_keep(v):
    return (v, None)

def back_low(kept, grad):
    return (low(grad),)
low.defvjp(low_keep, low_pass)
low_back.defvjp(back_keep, back_low)

def rms_scale(values):
    return lax.rsqrt(lax.optimization_barrier(jnp.mean(values * values, axis=-1, keepdims=True)) + EPS)

def scaled(values, gain_vec):
    return values * rms_scale(values) * gain_vec

def rope_tables(positions, head_width):
    halfway = head_width // 2
    frequency = THETA ** (-(jnp.arange(halfway, dtype=jnp.float32) * 2.0 / head_width))
    angles = positions.astype(jnp.float32)[:, None] * frequency[None, :]
    return (jnp.cos(angles), jnp.sin(angles))

def rotate(values, cos_table, sin_table):
    halfway = values.shape[-1] // 2
    first_half = values[..., :halfway]
    second_half = values[..., halfway:]
    return jnp.concatenate([first_half * cos_table - second_half * sin_table, second_half * cos_table + first_half * sin_table], axis=-1)

def query_piece(raw_proj, gain_vec, cos_table, sin_table):
    head_width = gain_vec.shape[0]
    per_head = raw_proj.reshape(raw_proj.shape[0], -1, head_width)
    normed = per_head * rms_scale(per_head) * gain_vec
    return rotate(normed, cos_table[:, None, :], sin_table[:, None, :]) * head_width ** (-0.5)

def key_piece(raw_proj, gain_vec, cos_table, sin_table):
    normed = raw_proj * rms_scale(raw_proj) * gain_vec
    return rotate(normed, cos_table, sin_table)

def positions_of(dealing_row, length_row, tok_rows):
    ctx_count = dealing_row.shape[0]
    offsets = jnp.arange(tok_rows, dtype=jnp.int32)
    halves = tok_rows // 2
    blocks = jnp.where(offsets[None, :] < halves, dealing_row[:, None], 2 * ctx_count - 1 - dealing_row[:, None])
    places = (blocks * halves + offsets[None, :] % halves).reshape(-1).astype(jnp.int32)
    first_len = length_row[0]
    second = places >= first_len
    in_seq = places - jnp.where(second, first_len, 0).astype(jnp.int32)
    return (places, second, in_seq)

def exact_dot(left_side, right_side):
    return jnp.dot(left_side, right_side, precision=lax.Precision.HIGHEST, preferred_element_type=jnp.float32)

def attend(queries, keys_all, values_all, places, second):
    group_rows = queries.shape[0]
    block_rows = math.gcd(group_rows, 512)
    block_count = group_rows // block_rows

    def one_block(block_args):
        query_block, place_block, second_block = block_args
        scores = low_back(jnp.einsum('qhd,kd->hqk', query_block, keys_all, precision=lax.Precision.HIGHEST))
        allowed = (second_block[:, None] == second[None, :]) & (places[None, :] <= place_block[:, None])
        scores = jnp.where(allowed[None], scores, -1e+30)
        log_total = jax.nn.logsumexp(scores, axis=-1, keepdims=True)
        prob_rows = low(jnp.exp(scores - log_total))
        return low(low_back(jnp.einsum('hqk,kd->qhd', prob_rows, values_all, precision=lax.Precision.HIGHEST)))
    result = lax.map(jax.checkpoint(one_block), (queries.reshape(block_count, block_rows, queries.shape[1], queries.shape[2]), places.reshape(block_count, block_rows), second.reshape(block_count, block_rows)))
    return result.reshape(group_rows, -1)

def block_layer(inputs, dealing_row, length_row, param_set):
    query_w, key_w, value_w, out_w, gate_w, up_w, down_w, input_gain, query_gain, key_gain, attn_gain, pre_gain, post_gain = param_set
    places, second, in_seq = positions_of(dealing_row, length_row, TOK_DEV)
    cos_table, sin_table = rope_tables(in_seq, HD)
    normed_in = low(scaled(inputs, input_gain))
    query_raw = low_back(exact_dot(normed_in, query_w))
    key_raw = low_back(exact_dot(normed_in, key_w))
    queries = low(query_piece(query_raw, query_gain, cos_table, sin_table))
    keys_all = low(key_piece(key_raw, key_gain, cos_table, sin_table))
    values_all = low(low_back(exact_dot(normed_in, value_w)))
    attended = attend(queries, keys_all, values_all, places, second)
    attn_proj = low_back(exact_dot(attended, out_w))
    hidden = inputs + scaled(attn_proj, attn_gain)
    normed_mid = low(scaled(hidden, pre_gain))
    gate_act = low_back(exact_dot(normed_mid, gate_w))
    up_act = low_back(exact_dot(normed_mid, up_w))
    glu_value = low(jax.nn.gelu(gate_act, approximate=True) * up_act)
    mlp_proj = low_back(exact_dot(glu_value, down_w))
    return hidden + scaled(mlp_proj, post_gain)

def reference(tokens, dealing, lengths, cotangent, query_proj, key_proj, value_proj, out_proj, gate_proj, up_proj, down_proj, gain_input, gain_query, gain_key, gain_attn, gain_pre, gain_post):
    params = tuple((weight_arr.astype(jnp.float32) for weight_arr in (query_proj, key_proj, value_proj, out_proj, gate_proj, up_proj, down_proj, gain_input, gain_query, gain_key, gain_attn, gain_pre, gain_post)))
    inputs = tokens.astype(jnp.float32)

    def forward(inputs_all, param_set):
        return jax.vmap(lambda one_input, one_deal, one_len: block_layer(one_input, one_deal, one_len, param_set))(inputs_all, dealing, lengths)
    outputs, pull_back = jax.vjp(forward, inputs, params)
    d_inputs, d_params = pull_back(cotangent.astype(jnp.float32))
    return (outputs.astype(jnp.bfloat16), d_inputs, d_params[0], d_params[1], d_params[2], d_params[3], d_params[4], d_params[5], d_params[6], d_params[7], d_params[8], d_params[9], d_params[10], d_params[11], d_params[12])
```

```python
import jax
import jax.numpy as jnp
from jax import lax
from jax.sharding import PartitionSpec as P

EPS = 1e-06
THETA = 1000000.0


def rms_scale(values):
    return lax.rsqrt(jnp.mean(values * values, axis=-1, keepdims=True) + EPS)


def scaled(values, gain_vec):
    return values * rms_scale(values) * gain_vec


def rope_tables(positions, head_width):
    halfway = head_width // 2
    frequency = THETA ** (-(jnp.arange(halfway, dtype=jnp.float32) * 2.0 / head_width))
    angles = positions.astype(jnp.float32)[:, None] * frequency[None, :]
    return (jnp.cos(angles), jnp.sin(angles))


def rotate(values, cos_table, sin_table):
    halfway = values.shape[-1] // 2
    first_half = values[..., :halfway]
    second_half = values[..., halfway:]
    return jnp.concatenate(
        [
            first_half * cos_table - second_half * sin_table,
            second_half * cos_table + first_half * sin_table,
        ],
        axis=-1,
    )


def query_piece(raw_proj, gain_vec, cos_table, sin_table):
    head_width = gain_vec.shape[0]
    per_head = raw_proj.reshape(raw_proj.shape[0], -1, head_width)
    normed = per_head * rms_scale(per_head) * gain_vec
    return rotate(normed, cos_table[:, None, :], sin_table[:, None, :]) * head_width ** (-0.5)


def key_piece(raw_proj, gain_vec, cos_table, sin_table):
    normed = raw_proj * rms_scale(raw_proj) * gain_vec
    return rotate(normed, cos_table, sin_table)


def positions_of(dealing_row, length_row, tok_rows):
    ctx_count = dealing_row.shape[0]
    offsets = jnp.arange(tok_rows, dtype=jnp.int32)
    halves = tok_rows // 2
    blocks = jnp.where(
        offsets[None, :] < halves, dealing_row[:, None], 2 * ctx_count - 1 - dealing_row[:, None]
    )
    places = (blocks * halves + offsets[None, :] % halves).reshape(-1)
    first_len = length_row[0]
    second = places >= first_len
    in_seq = places - jnp.where(second, first_len, 0)
    return (places, second, in_seq)


def dot_last(left_side, right_side):
    return lax.dot_general(
        left_side, right_side, (((1,), (1,)), ((), ())), preferred_element_type=jnp.float32
    )


def dot_first(left_side, right_side):
    return lax.dot_general(
        left_side, right_side, (((0,), (0,)), ((), ())), preferred_element_type=jnp.float32
    )


def per_device(
    tokens,
    dealing,
    lengths,
    cotangent,
    query_proj,
    key_proj,
    value_proj,
    out_proj,
    gate_proj,
    up_proj,
    down_proj,
    gain_input,
    gain_query,
    gain_key,
    gain_attn,
    gain_pre,
    gain_post,
):
    ctx_count = dealing.shape[1]
    fsdp_count = lax.axis_size("fsdp")
    ctx_index = lax.axis_index("ctx")
    tok_rows, width = tokens.shape[1], tokens.shape[2]
    head_cols = query_proj.shape[1]
    head_width = key_proj.shape[1]
    qkv_cols = head_cols + 2 * head_width

    qkv_own = jnp.concatenate([query_proj, key_proj, value_proj], axis=1)
    qkv_piece = qkv_own.shape[0] // ctx_count
    gains_own = jnp.concatenate(
        [gain_input, gain_query, gain_key, gain_attn, gain_pre, gain_post]
    )
    gain_sizes = [
        v.shape[0] for v in (gain_input, gain_query, gain_key, gain_attn, gain_pre, gain_post)
    ]
    gain_row = jnp.pad(gains_own, (0, qkv_cols - gains_own.shape[0]))[None]
    qkv_send = jnp.concatenate(
        [lax.dynamic_slice_in_dim(qkv_own, ctx_index * qkv_piece, qkv_piece), gain_row], axis=0
    )
    qkv_got = lax.all_gather(qkv_send, ("fsdp", "ctx"), axis=0).reshape(
        fsdp_count, ctx_count, qkv_piece + 1, qkv_cols
    )
    qkv_full = qkv_got[:, :, :qkv_piece].reshape(-1, qkv_cols)
    gains_got = qkv_got[:, 0, qkv_piece].astype(jnp.float32)
    gain_full = []
    at = 0
    for size in gain_sizes:
        gain_full.append(gains_got[:, at : at + size].reshape(-1))
        at += size
    input_gain, query_gain, key_gain, attn_gain, pre_gain, post_gain = gain_full
    out_piece = out_proj.shape[0] // ctx_count
    out_full = lax.all_gather(
        lax.dynamic_slice_in_dim(out_proj, ctx_index * out_piece, out_piece),
        ("fsdp", "ctx"),
        axis=0,
        tiled=True,
    )

    unit_rows = down_proj.shape[0]
    unit_piece = unit_rows // ctx_count
    unit_own = fsdp_count * unit_piece
    unit_pad = -(-unit_own // 128) * 128

    def unit_columns(weight):
        parts = [
            lax.dynamic_slice_in_dim(
                weight, index * unit_rows + ctx_index * unit_piece, unit_piece, axis=1
            )
            for index in range(fsdp_count)
        ]
        parts.append(jnp.zeros((weight.shape[0], unit_pad - unit_own), weight.dtype))
        return jnp.concatenate(parts, axis=1)

    gate_up = lax.all_gather(
        jnp.concatenate([unit_columns(gate_proj), unit_columns(up_proj)], axis=1),
        "fsdp",
        axis=0,
        tiled=True,
    )
    down_own = lax.all_gather(
        lax.dynamic_slice_in_dim(down_proj, ctx_index * unit_piece, unit_piece),
        "fsdp",
        axis=0,
        tiled=True,
    )
    down_own = jnp.pad(down_own, ((0, unit_pad - unit_own), (0, 0)))

    places, second, in_seq = positions_of(dealing[0], lengths[0], tok_rows)
    row_start = ctx_index * tok_rows
    own_place = lax.dynamic_slice_in_dim(places, row_start, tok_rows)
    own_second = lax.dynamic_slice_in_dim(second, row_start, tok_rows)
    own_seq = lax.dynamic_slice_in_dim(in_seq, row_start, tok_rows)
    allowed = (own_second[:, None] == second[None, :]) & (places[None, :] <= own_place[:, None])
    cos_table, sin_table = rope_tables(own_seq, head_width)
    inputs = tokens[0].astype(jnp.float32)
    normed_in, in_pull = jax.vjp(scaled, inputs, input_gain)
    normed_bf = normed_in.astype(jnp.bfloat16)
    qkv_raw = jnp.dot(normed_bf, qkv_full, preferred_element_type=jnp.float32)
    query_raw = qkv_raw[:, :head_cols]
    key_raw = qkv_raw[:, head_cols : head_cols + head_width]
    value_raw = qkv_raw[:, head_cols + head_width :]
    query_rot, query_pull = jax.vjp(
        lambda raw_proj, gain_vec: query_piece(raw_proj, gain_vec, cos_table, sin_table),
        query_raw,
        query_gain,
    )
    key_rot, key_pull = jax.vjp(
        lambda raw_proj, gain_vec: key_piece(raw_proj, gain_vec, cos_table, sin_table),
        key_raw,
        key_gain,
    )
    query_rows = jnp.transpose(query_rot.astype(jnp.bfloat16), (1, 0, 2)).reshape(-1, head_width)
    kv_all = lax.all_gather(
        jnp.concatenate([key_rot, value_raw], axis=1).astype(jnp.bfloat16),
        "ctx",
        axis=0,
        tiled=True,
    )
    key_all, value_all = kv_all[:, :head_width], kv_all[:, head_width:]
    heads = head_cols // head_width
    scores = dot_last(query_rows, key_all).reshape(heads, tok_rows, -1)
    weights = jnp.where(allowed[None], jnp.exp(scores), 0.0)
    totals = jnp.sum(weights, axis=-1, keepdims=True)
    probs_bf = (weights * (1.0 / totals)).astype(jnp.bfloat16).reshape(heads * tok_rows, -1)
    attn_heads = jnp.dot(probs_bf, value_all, preferred_element_type=jnp.float32).reshape(
        heads, tok_rows, head_width
    )
    attn_bf = jnp.transpose(attn_heads, (1, 0, 2)).reshape(tok_rows, -1).astype(jnp.bfloat16)
    attn_proj = jnp.dot(attn_bf, out_full, preferred_element_type=jnp.float32)
    attn_normed, attn_pull = jax.vjp(scaled, attn_proj, attn_gain)
    hidden = inputs + attn_normed
    normed_mid, mid_pull = jax.vjp(scaled, hidden, pre_gain)
    mid_all = lax.all_gather(normed_mid.astype(jnp.bfloat16), "ctx", axis=0, tiled=True)
    gate_up_act = jnp.dot(mid_all, gate_up, preferred_element_type=jnp.float32)
    gate_act, up_act = gate_up_act[:, :unit_pad], gate_up_act[:, unit_pad:]
    glu_value, glu_pull = jax.vjp(
        lambda gate_in, up_in: jax.nn.gelu(gate_in, approximate=True) * up_in, gate_act, up_act
    )
    glu_bf = glu_value.astype(jnp.bfloat16)
    mlp_part = jnp.dot(glu_bf, down_own, preferred_element_type=jnp.float32)
    mlp_proj = lax.psum_scatter(
        mlp_part.astype(jnp.bfloat16), "ctx", scatter_dimension=0, tiled=True
    ).astype(jnp.float32)
    post_value, post_pull = jax.vjp(scaled, mlp_proj, post_gain)
    outputs_bf = (hidden + post_value).astype(jnp.bfloat16)
    d_out = cotangent[0].astype(jnp.float32)
    d_mlp, d_post_gain = post_pull(d_out)
    d_mlp_all = lax.all_gather(d_mlp.astype(jnp.bfloat16), "ctx", axis=0, tiled=True)
    d_glu = dot_last(d_mlp_all, down_own)
    d_gate, d_up = glu_pull(d_glu)
    d_gate_up = jnp.concatenate([d_gate, d_up], axis=1).astype(jnp.bfloat16)
    d_mid_part = dot_last(d_gate_up, gate_up)
    d_mid = lax.psum_scatter(
        d_mid_part.astype(jnp.bfloat16), "ctx", scatter_dimension=0, tiled=True
    ).astype(jnp.float32)
    grad_down = dot_first(glu_bf, d_mlp_all)[:unit_own].astype(jnp.bfloat16)
    grad_gate_up = dot_first(mid_all, d_gate_up).astype(jnp.bfloat16)
    grad_down = lax.psum_scatter(grad_down, "fsdp", scatter_dimension=0, tiled=True)
    grad_gate_up = lax.psum_scatter(grad_gate_up, "fsdp", scatter_dimension=0, tiled=True)
    grad_down = lax.all_gather(grad_down, "ctx", axis=0, tiled=True).astype(jnp.float32)
    grad_gate_up = lax.all_gather(grad_gate_up, "ctx", axis=0)

    def unit_order(pieces):
        rows = pieces.shape[1]
        pieces = pieces.reshape(ctx_count, rows, fsdp_count, unit_piece)
        return jnp.transpose(pieces, (1, 2, 0, 3)).reshape(rows, -1).astype(jnp.float32)

    grad_gate = unit_order(grad_gate_up[:, :, :unit_own])
    grad_up = unit_order(grad_gate_up[:, :, unit_pad : unit_pad + unit_own])
    d_hidden_part, d_pre_gain = mid_pull(d_mid)
    d_hidden = d_out + d_hidden_part
    d_attn_proj, d_attn_gain = attn_pull(d_hidden)
    d_proj_bf = d_attn_proj.astype(jnp.bfloat16)
    grad_out = lax.psum_scatter(
        dot_first(attn_bf, d_proj_bf).astype(jnp.bfloat16),
        ("fsdp", "ctx"),
        scatter_dimension=0,
        tiled=True,
    )
    grad_out = lax.all_gather(grad_out, "ctx", axis=0, tiled=True).astype(jnp.float32)
    d_attn_bf = dot_last(d_proj_bf, out_full).astype(jnp.bfloat16)
    d_rows = jnp.transpose(d_attn_bf.reshape(tok_rows, -1, head_width), (1, 0, 2)).reshape(
        -1, head_width
    )
    d_probs = dot_last(d_rows, value_all)
    probs = probs_bf.astype(jnp.float32)
    inner_sum = jnp.sum(probs * d_probs, axis=-1, keepdims=True)
    d_scores = (probs * (d_probs - inner_sum)).astype(jnp.bfloat16)
    key_grad = dot_first(d_scores, query_rows)
    value_grad = dot_first(probs_bf, d_rows)
    kv_own = lax.psum_scatter(
        jnp.concatenate([key_grad, value_grad], axis=1).astype(jnp.bfloat16),
        "ctx",
        scatter_dimension=0,
        tiled=True,
    ).astype(jnp.float32)
    d_query = jnp.transpose(
        jnp.dot(d_scores, key_all, preferred_element_type=jnp.float32).reshape(
            heads, tok_rows, head_width
        ),
        (1, 0, 2),
    )
    d_query_raw, d_query_gain = query_pull(d_query)
    d_key_raw, d_key_gain = key_pull(kv_own[:, :head_width])
    d_qkv_bf = jnp.concatenate([d_query_raw, d_key_raw, kv_own[:, head_width:]], axis=1).astype(
        jnp.bfloat16
    )
    d_normed = dot_last(d_qkv_bf, qkv_full)
    d_inputs_part, d_input_gain = in_pull(d_normed)
    d_inputs = d_hidden + d_inputs_part
    grad_qkv = dot_first(normed_bf, d_qkv_bf).astype(jnp.bfloat16)
    gain_grads = jnp.concatenate(
        [
            v.reshape(fsdp_count, -1)
            for v in (
                d_input_gain,
                d_query_gain,
                d_key_gain,
                d_attn_gain,
                d_pre_gain,
                d_post_gain,
            )
        ],
        axis=1,
    ).astype(jnp.bfloat16)
    gain_grads = jnp.pad(gain_grads, ((0, 0), (0, qkv_cols - gain_grads.shape[1])))
    qkv_terms = jnp.concatenate(
        [
            grad_qkv.reshape(fsdp_count, ctx_count, qkv_piece, qkv_cols),
            jnp.broadcast_to(
                gain_grads[:, None, None], (fsdp_count, ctx_count, 1, qkv_cols)
            ),
        ],
        axis=2,
    ).reshape(fsdp_count * ctx_count, qkv_piece + 1, qkv_cols)
    qkv_sum = lax.psum_scatter(qkv_terms, ("fsdp", "ctx"), scatter_dimension=0, tiled=True)[0]
    gain_sum = qkv_sum[qkv_piece].astype(jnp.float32)
    grad_qkv = lax.all_gather(qkv_sum[:qkv_piece], "ctx", axis=0, tiled=True).astype(jnp.float32)
    gain_out = []
    at = 0
    for size in gain_sizes:
        gain_out.append(gain_sum[at : at + size])
        at += size
    return (
        outputs_bf[None],
        d_inputs[None],
        grad_qkv[:, :head_cols],
        grad_qkv[:, head_cols : head_cols + head_width],
        grad_qkv[:, head_cols + head_width :],
        grad_out,
        grad_gate,
        grad_up,
        grad_down,
        *gain_out,
    )


def solution(mesh):
    return jax.shard_map(
        per_device,
        mesh=mesh,
        in_specs=(
            P("fsdp", "ctx", None),
            P("fsdp", None),
            P("fsdp", None),
            P("fsdp", "ctx", None),
            P("fsdp", None),
            P("fsdp", None),
            P("fsdp", None),
            P("fsdp", None),
            P("fsdp", None),
            P("fsdp", None),
            P("fsdp", None),
            P("fsdp"),
            P("fsdp"),
            P("fsdp"),
            P("fsdp"),
            P("fsdp"),
            P("fsdp"),
        ),
        out_specs=(
            P("fsdp", "ctx", None),
            P("fsdp", "ctx", None),
            P("fsdp", None),
            P("fsdp", None),
            P("fsdp", None),
            P("fsdp", None),
            P("fsdp", None),
            P("fsdp", None),
            P("fsdp", None),
            P("fsdp"),
            P("fsdp"),
            P("fsdp"),
            P("fsdp"),
            P("fsdp"),
            P("fsdp"),
        ),
        check_vma=False,
    )
```

```python
import jax
import jax.numpy as jnp
from jax import lax
from jax.experimental import pallas as pl
from jax.experimental.pallas import tpu as pltpu
from jax.sharding import PartitionSpec as P

EPS = 1e-06
THETA = 1000000.0


def rms_scale(values):
    return lax.rsqrt(jnp.mean(values * values, axis=-1, keepdims=True) + EPS)


def scaled(values, gain_vec):
    return values * rms_scale(values) * gain_vec


def rope_tables(positions, head_width):
    halfway = head_width // 2
    frequency = THETA ** (-(jnp.arange(halfway, dtype=jnp.float32) * 2.0 / head_width))
    angles = positions.astype(jnp.float32)[:, None] * frequency[None, :]
    return (jnp.cos(angles), jnp.sin(angles))


def rotate(values, cos_table, sin_table):
    halfway = values.shape[-1] // 2
    first_half = values[..., :halfway]
    second_half = values[..., halfway:]
    return jnp.concatenate(
        [
            first_half * cos_table - second_half * sin_table,
            second_half * cos_table + first_half * sin_table,
        ],
        axis=-1,
    )


def query_piece(raw_proj, gain_vec, cos_table, sin_table):
    head_width = gain_vec.shape[0]
    per_head = raw_proj.reshape(raw_proj.shape[0], -1, head_width)
    normed = per_head * rms_scale(per_head) * gain_vec
    return rotate(normed, cos_table[:, None, :], sin_table[:, None, :]) * head_width ** (-0.5)


def key_piece(raw_proj, gain_vec, cos_table, sin_table):
    normed = raw_proj * rms_scale(raw_proj) * gain_vec
    return rotate(normed, cos_table, sin_table)


def positions_of(dealing_row, length_row, tok_rows):
    ctx_count = dealing_row.shape[0]
    offsets = jnp.arange(tok_rows, dtype=jnp.int32)
    halves = tok_rows // 2
    blocks = jnp.where(
        offsets[None, :] < halves, dealing_row[:, None], 2 * ctx_count - 1 - dealing_row[:, None]
    )
    places = (blocks * halves + offsets[None, :] % halves).reshape(-1)
    first_len = length_row[0]
    second = places >= first_len
    in_seq = places - jnp.where(second, first_len, 0)
    return (places, second, in_seq)


def dot_last(left_side, right_side):
    return lax.dot_general(
        left_side, right_side, (((1,), (1,)), ((), ())), preferred_element_type=jnp.float32
    )


def dot_first(left_side, right_side):
    return lax.dot_general(
        left_side, right_side, (((0,), (0,)), ((), ())), preferred_element_type=jnp.float32
    )


def shifted(values, step, count):
    return lax.ppermute(values, "fsdp", [(i, (i + step) % count) for i in range(count)])


def send_piece(piece):
    count = lax.axis_size("fsdp")
    return [shifted(piece, step, count) for step in range(1, count)]


def stack_pieces(piece, received):
    count = lax.axis_size("fsdp")
    me = lax.axis_index("fsdp")
    whole = jnp.zeros((count, *piece.shape), piece.dtype)
    whole = lax.dynamic_update_index_in_dim(whole, piece, me, 0)
    for step, got in enumerate(received, 1):
        whole = lax.dynamic_update_index_in_dim(whole, got, lax.rem(me - step + count, count), 0)
    return whole


def gather_fsdp(piece):
    return stack_pieces(piece, send_piece(piece))


def after(value, received, index):
    value, received[index] = lax.optimization_barrier((value, received[index]))
    return value


def send_chunks(chunks):
    count = lax.axis_size("fsdp")
    me = lax.axis_index("fsdp")
    received = []
    for step in range(1, count):
        sent = lax.dynamic_index_in_dim(chunks, lax.rem(me + step, count), 0, keepdims=False)
        received.append(shifted(sent, step, count))
    return received


def own_total(chunks, received):
    me = lax.axis_index("fsdp")
    total = lax.dynamic_index_in_dim(chunks, me, 0, keepdims=False).astype(jnp.float32)
    for got in received:
        total = total + got.astype(jnp.float32)
    return total


def sum_fsdp(chunks):
    return own_total(chunks, send_chunks(chunks))


def unit_order(pieces, fsdp_count, unit_piece, unit_pad):
    ctx_count, rows, cols = pieces.shape
    units = ctx_count * fsdp_count * unit_piece
    block = 32 if rows % 32 == 0 else rows

    def kernel(in_ref, gate_ref, up_ref):
        for out_ref, base in ((gate_ref, 0), (up_ref, unit_pad)):
            held = [
                in_ref[c, :, base : base + unit_pad].astype(jnp.float32) for c in range(ctx_count)
            ]
            for pair in range(fsdp_count // 2):
                parts = [
                    held[c][:, f * unit_piece : (f + 1) * unit_piece]
                    for f in (2 * pair, 2 * pair + 1)
                    for c in range(ctx_count)
                ]
                span = units * 2 // fsdp_count
                out_ref[:, pair * span : (pair + 1) * span] = jnp.concatenate(parts, axis=1)

    return pl.pallas_call(
        kernel,
        grid=(rows // block,),
        in_specs=[pl.BlockSpec((ctx_count, block, cols), lambda i: (0, i, 0))],
        out_specs=[pl.BlockSpec((block, units), lambda i: (i, 0))] * 2,
        out_shape=[jax.ShapeDtypeStruct((rows, units), jnp.float32)] * 2,
        compiler_params=pltpu.CompilerParams(vmem_limit_bytes=40 * 1024 * 1024),
    )(pieces)


def per_device(
    tokens,
    dealing,
    lengths,
    cotangent,
    query_proj,
    key_proj,
    value_proj,
    out_proj,
    gate_proj,
    up_proj,
    down_proj,
    gain_input,
    gain_query,
    gain_key,
    gain_attn,
    gain_pre,
    gain_post,
):
    ctx_count = dealing.shape[1]
    fsdp_count = lax.axis_size("fsdp")
    ctx_index = lax.axis_index("ctx")
    tok_rows, width = tokens.shape[1], tokens.shape[2]
    head_cols = query_proj.shape[1]
    head_width = key_proj.shape[1]
    qkv_cols = head_cols + 2 * head_width

    qkv_own = jnp.concatenate([query_proj, key_proj, value_proj], axis=1)
    qkv_piece = qkv_own.shape[0] // ctx_count
    gains_own = jnp.concatenate(
        [gain_input, gain_query, gain_key, gain_attn, gain_pre, gain_post]
    )
    gain_sizes = [
        v.shape[0] for v in (gain_input, gain_query, gain_key, gain_attn, gain_pre, gain_post)
    ]
    gain_row = jnp.pad(gains_own, (0, qkv_cols - gains_own.shape[0]))[None]
    qkv_send = jnp.concatenate(
        [lax.dynamic_slice_in_dim(qkv_own, ctx_index * qkv_piece, qkv_piece), gain_row], axis=0
    )
    qkv_layers = gather_fsdp(qkv_send)
    gains_got = qkv_layers[:, qkv_piece].astype(jnp.float32)
    qkv_got = lax.all_gather(qkv_layers[:, :qkv_piece], "ctx", axis=0)
    qkv_full = jnp.transpose(qkv_got, (1, 0, 2, 3)).reshape(-1, qkv_cols)
    gain_full = []
    at = 0
    for size in gain_sizes:
        gain_full.append(gains_got[:, at : at + size].reshape(-1))
        at += size
    input_gain, query_gain, key_gain, attn_gain, pre_gain, post_gain = gain_full
    out_piece = out_proj.shape[0] // ctx_count
    out_layers = gather_fsdp(
        lax.dynamic_slice_in_dim(out_proj, ctx_index * out_piece, out_piece)
    )
    out_got = lax.all_gather(out_layers, "ctx", axis=0)
    out_full = jnp.transpose(out_got, (1, 0, 2, 3)).reshape(-1, width)

    unit_rows = down_proj.shape[0]
    unit_piece = unit_rows // ctx_count
    unit_own = fsdp_count * unit_piece
    unit_pad = -(-unit_own // 128) * 128

    def unit_columns(weight):
        parts = [
            lax.dynamic_slice_in_dim(
                weight, index * unit_rows + ctx_index * unit_piece, unit_piece, axis=1
            )
            for index in range(fsdp_count)
        ]
        parts.append(jnp.zeros((weight.shape[0], unit_pad - unit_own), weight.dtype))
        return jnp.concatenate(parts, axis=1)

    gate_up_own = jnp.concatenate([unit_columns(gate_proj), unit_columns(up_proj)], axis=1)
    gate_up_got = send_piece(gate_up_own)
    down_own = gather_fsdp(
        lax.dynamic_slice_in_dim(down_proj, ctx_index * unit_piece, unit_piece)
    ).reshape(unit_own, width)
    down_own = jnp.pad(down_own, ((0, unit_pad - unit_own), (0, 0)))

    places, second, in_seq = positions_of(dealing[0], lengths[0], tok_rows)
    row_start = ctx_index * tok_rows
    own_place = lax.dynamic_slice_in_dim(places, row_start, tok_rows)
    own_second = lax.dynamic_slice_in_dim(second, row_start, tok_rows)
    own_seq = lax.dynamic_slice_in_dim(in_seq, row_start, tok_rows)
    allowed = (own_second[:, None] == second[None, :]) & (places[None, :] <= own_place[:, None])
    cos_table, sin_table = rope_tables(own_seq, head_width)
    inputs = tokens[0].astype(jnp.float32)
    normed_in, in_pull = jax.vjp(scaled, inputs, input_gain)
    normed_bf = normed_in.astype(jnp.bfloat16)
    qkv_raw = jnp.dot(normed_bf, qkv_full, preferred_element_type=jnp.float32)
    query_raw = qkv_raw[:, :head_cols]
    key_raw = qkv_raw[:, head_cols : head_cols + head_width]
    value_raw = qkv_raw[:, head_cols + head_width :]
    query_rot, query_pull = jax.vjp(
        lambda raw_proj, gain_vec: query_piece(raw_proj, gain_vec, cos_table, sin_table),
        query_raw,
        query_gain,
    )
    key_rot, key_pull = jax.vjp(
        lambda raw_proj, gain_vec: key_piece(raw_proj, gain_vec, cos_table, sin_table),
        key_raw,
        key_gain,
    )
    query_rows = jnp.transpose(query_rot.astype(jnp.bfloat16), (1, 0, 2)).reshape(-1, head_width)
    kv_all = lax.all_gather(
        jnp.concatenate([key_rot, value_raw], axis=1).astype(jnp.bfloat16),
        "ctx",
        axis=0,
        tiled=True,
    )
    key_all, value_all = kv_all[:, :head_width], kv_all[:, head_width:]
    heads = head_cols // head_width
    query_rows = after(query_rows, gate_up_got, 0)
    scores = dot_last(query_rows, key_all).reshape(heads, tok_rows, -1)
    weights = jnp.where(allowed[None], jnp.exp(scores), 0.0)
    totals = jnp.sum(weights, axis=-1, keepdims=True)
    probs_bf = (weights * (1.0 / totals)).astype(jnp.bfloat16).reshape(heads * tok_rows, -1)
    attn_heads = jnp.dot(probs_bf, value_all, preferred_element_type=jnp.float32).reshape(
        heads, tok_rows, head_width
    )
    attn_bf = jnp.transpose(attn_heads, (1, 0, 2)).reshape(tok_rows, -1).astype(jnp.bfloat16)
    attn_bf = after(attn_bf, gate_up_got, 1)
    attn_proj = jnp.dot(attn_bf, out_full, preferred_element_type=jnp.float32)
    attn_normed, attn_pull = jax.vjp(scaled, attn_proj, attn_gain)
    hidden = inputs + attn_normed
    normed_mid, mid_pull = jax.vjp(scaled, hidden, pre_gain)
    mid_all = lax.all_gather(normed_mid.astype(jnp.bfloat16), "ctx", axis=0, tiled=True)
    gate_up = stack_pieces(gate_up_own, gate_up_got).reshape(width, 2 * unit_pad)
    gate_up_act = jnp.dot(mid_all, gate_up, preferred_element_type=jnp.float32)
    gate_act, up_act = gate_up_act[:, :unit_pad], gate_up_act[:, unit_pad:]
    glu_value, glu_pull = jax.vjp(
        lambda gate_in, up_in: jax.nn.gelu(gate_in, approximate=True) * up_in, gate_act, up_act
    )
    glu_bf = glu_value.astype(jnp.bfloat16)
    mlp_part = jnp.dot(glu_bf, down_own, preferred_element_type=jnp.float32)
    mlp_proj = lax.psum_scatter(
        mlp_part.astype(jnp.bfloat16), "ctx", scatter_dimension=0, tiled=True
    ).astype(jnp.float32)
    post_value, post_pull = jax.vjp(scaled, mlp_proj, post_gain)
    outputs_bf = (hidden + post_value).astype(jnp.bfloat16)
    d_out = cotangent[0].astype(jnp.float32)
    d_mlp, d_post_gain = post_pull(d_out)
    d_mlp_all = lax.all_gather(d_mlp.astype(jnp.bfloat16), "ctx", axis=0, tiled=True)
    d_glu = dot_last(d_mlp_all, down_own)
    d_gate, d_up = glu_pull(d_glu)
    d_gate_up = jnp.concatenate([d_gate, d_up], axis=1).astype(jnp.bfloat16)
    d_mid_part = dot_last(d_gate_up, gate_up)
    d_mid = lax.psum_scatter(
        d_mid_part.astype(jnp.bfloat16), "ctx", scatter_dimension=0, tiled=True
    ).astype(jnp.float32)
    grad_down = dot_first(glu_bf, d_mlp_all)[:unit_own].astype(jnp.bfloat16)
    grad_gate_up = dot_first(mid_all, d_gate_up).astype(jnp.bfloat16)
    grad_down_chunks = grad_down.reshape(fsdp_count, unit_piece, width)
    grad_gate_up_chunks = grad_gate_up.reshape(fsdp_count, -1, 2 * unit_pad)
    grad_down_got = send_chunks(grad_down_chunks)
    grad_gate_up_got = send_chunks(grad_gate_up_chunks)
    d_mid, _, _ = lax.optimization_barrier((d_mid, grad_down, grad_gate_up))
    d_hidden_part, d_pre_gain = mid_pull(d_mid)
    d_hidden = d_out + d_hidden_part
    d_attn_proj, d_attn_gain = attn_pull(d_hidden)
    d_proj_bf = d_attn_proj.astype(jnp.bfloat16)
    out_terms = dot_first(attn_bf, d_proj_bf).astype(jnp.bfloat16)
    out_terms = jnp.transpose(
        out_terms.reshape(fsdp_count, ctx_count, out_piece, width), (1, 0, 2, 3)
    ).reshape(-1, width)
    out_sum = lax.psum_scatter(out_terms, "ctx", scatter_dimension=0, tiled=True)
    grad_out = sum_fsdp(out_sum.reshape(fsdp_count, out_piece, width)).astype(jnp.bfloat16)
    grad_out = lax.all_gather(grad_out, "ctx", axis=0, tiled=True).astype(jnp.float32)
    d_attn_bf = dot_last(d_proj_bf, out_full).astype(jnp.bfloat16)
    d_rows = jnp.transpose(d_attn_bf.reshape(tok_rows, -1, head_width), (1, 0, 2)).reshape(
        -1, head_width
    )
    d_probs = dot_last(d_rows, value_all)
    probs = probs_bf.astype(jnp.float32)
    inner_sum = jnp.sum(probs * d_probs, axis=-1, keepdims=True)
    d_scores = (probs * (d_probs - inner_sum)).astype(jnp.bfloat16)
    key_grad = dot_first(d_scores, query_rows)
    value_grad = dot_first(probs_bf, d_rows)
    kv_terms = jnp.concatenate([key_grad, value_grad], axis=1).astype(jnp.bfloat16)
    kv_terms = after(kv_terms, grad_gate_up_got, 0)
    kv_own = lax.psum_scatter(
        kv_terms,
        "ctx",
        scatter_dimension=0,
        tiled=True,
    ).astype(jnp.float32)
    d_query = jnp.transpose(
        jnp.dot(d_scores, key_all, preferred_element_type=jnp.float32).reshape(
            heads, tok_rows, head_width
        ),
        (1, 0, 2),
    )
    d_query_raw, d_query_gain = query_pull(d_query)
    kv_own = after(kv_own, grad_gate_up_got, 1)
    d_key_raw, d_key_gain = key_pull(kv_own[:, :head_width])
    d_qkv_bf = jnp.concatenate([d_query_raw, d_key_raw, kv_own[:, head_width:]], axis=1).astype(
        jnp.bfloat16
    )
    d_normed = dot_last(d_qkv_bf, qkv_full)
    d_inputs_part, d_input_gain = in_pull(d_normed)
    d_inputs = d_hidden + d_inputs_part
    grad_qkv = dot_first(normed_bf, d_qkv_bf).astype(jnp.bfloat16)
    gain_grads = jnp.concatenate(
        [
            v.reshape(fsdp_count, -1)
            for v in (
                d_input_gain,
                d_query_gain,
                d_key_gain,
                d_attn_gain,
                d_pre_gain,
                d_post_gain,
            )
        ],
        axis=1,
    ).astype(jnp.bfloat16)
    gain_grads = jnp.pad(gain_grads, ((0, 0), (0, qkv_cols - gain_grads.shape[1])))
    qkv_slot = -(-(qkv_piece + 1) // 8) * 8
    qkv_terms = jnp.concatenate(
        [
            grad_qkv.reshape(fsdp_count, ctx_count, qkv_piece, qkv_cols),
            jnp.broadcast_to(
                gain_grads[:, None, None], (fsdp_count, ctx_count, 1, qkv_cols)
            ),
            jnp.zeros(
                (fsdp_count, ctx_count, qkv_slot - qkv_piece - 1, qkv_cols), jnp.bfloat16
            ),
        ],
        axis=2,
    )
    qkv_terms = jnp.transpose(qkv_terms, (1, 0, 2, 3)).reshape(-1, qkv_cols)
    qkv_terms = after(qkv_terms, grad_gate_up_got, 2)
    qkv_sum = lax.psum_scatter(qkv_terms, "ctx", scatter_dimension=0, tiled=True)
    qkv_sum = sum_fsdp(qkv_sum.reshape(fsdp_count, qkv_slot, qkv_cols)[:, : qkv_piece + 1])
    gain_sum = qkv_sum[qkv_piece]
    grad_qkv = lax.all_gather(
        qkv_sum[:qkv_piece].astype(jnp.bfloat16), "ctx", axis=0, tiled=True
    ).astype(jnp.float32)
    grad_down = own_total(grad_down_chunks, grad_down_got).astype(jnp.bfloat16)
    grad_gate_up = own_total(grad_gate_up_chunks, grad_gate_up_got).astype(jnp.bfloat16)
    grad_down = lax.all_gather(grad_down, "ctx", axis=0, tiled=True).astype(jnp.float32)
    grad_gate, grad_up = unit_order(
        lax.all_gather(grad_gate_up, "ctx", axis=0), fsdp_count, unit_piece, unit_pad
    )
    gain_out = []
    at = 0
    for size in gain_sizes:
        gain_out.append(gain_sum[at : at + size])
        at += size
    return (
        outputs_bf[None],
        d_inputs[None],
        grad_qkv[:, :head_cols],
        grad_qkv[:, head_cols : head_cols + head_width],
        grad_qkv[:, head_cols + head_width :],
        grad_out,
        grad_gate,
        grad_up,
        grad_down,
        *gain_out,
    )


def solution(mesh):
    return jax.shard_map(
        per_device,
        mesh=mesh,
        in_specs=(
            P("fsdp", "ctx", None),
            P("fsdp", None),
            P("fsdp", None),
            P("fsdp", "ctx", None),
            P("fsdp", None),
            P("fsdp", None),
            P("fsdp", None),
            P("fsdp", None),
            P("fsdp", None),
            P("fsdp", None),
            P("fsdp", None),
            P("fsdp"),
            P("fsdp"),
            P("fsdp"),
            P("fsdp"),
            P("fsdp"),
            P("fsdp"),
        ),
        out_specs=(
            P("fsdp", "ctx", None),
            P("fsdp", "ctx", None),
            P("fsdp", None),
            P("fsdp", None),
            P("fsdp", None),
            P("fsdp", None),
            P("fsdp", None),
            P("fsdp", None),
            P("fsdp", None),
            P("fsdp"),
            P("fsdp"),
            P("fsdp"),
            P("fsdp"),
            P("fsdp"),
            P("fsdp"),
        ),
        check_vma=False,
    )
```
